32 devices in a mesh: bead: 2 (over y), row: 4 (over x, core), col: 4 (over z).
Axes of the slice: x: 2, y: 2, z: 4, core: 2. Of those that a mesh axis runs over, the one named last changes fastest.
Arguments:
- tensor_tiles: bfloat16 [256, 3, 128, 3, 128], P(('bead', 'row', 'col')), parts along dimension 0, may hold values from -0.02734375 to 0.02734375
- pair_blocks: int32 [256, 2], P(('bead', 'row', 'col')), parts along dimension 0, may hold values from 0 to 31, as said below
- polarizability: float32 [4096], P('row'), may hold values from 0.3 to 1.2
- direct_field: float32 [3, 8192], P(None, ('bead', 'row')), parts along dimension 1, may hold values from -6 to 6
- cotangent: float32 [3, 8192], P(None, ('bead', 'row')), parts along dimension 1, may hold values from -6 to 6
Outputs:
- dipoles: float32 [3, 8192], P(None, ('bead', 'row')), parts along dimension 1
- field_grad: float32 [3, 8192], P(None, ('bead', 'row')), parts along dimension 1
- tile_grad: bfloat16 [256, 3, 128, 3, 128], P(('bead', 'row', 'col')), parts along dimension 0
The draws below stay inside these ranges and needn't reach their ends.
There are 2 independent parts, one for each index of `bead`. The reference program is written for one: setup_inputs(seed, part) draws one part's arguments, and reference() takes and returns one part's arrays. A program takes and returns all parts, laid end to end along the dimension named above; an argument that names none is the same for every part. Nothing has to cross between parts.
Inputs may be any that keep to these rules, and one draw needn't show every extreme that they name: `pair_blocks`: for pair p, with d = p // 8, the first block lies in [(d // 4) * 8, (d // 4 + 1) * 8) and below 31; the second block is larger than the first.
All inputs are finite; a program needn't handle non-finite values.
Results may differ from the reference program's by a relative error of at most 0.0057.
Values may be sent and summed in bfloat16 or wider, within the bound.
A program may use at most 64 MiB of HBM per device.

```python
import math
import jax
import jax.numpy as jnp
from jax import lax

BLOCK = 128
BR = 8
PD = 8
ITERS = 3
NB = 32
NA = 4096
NP = 128
N_ROW = 4
N_COL = 4


def draw_pair_blocks(key, part):
    key = jax.random.fold_in(key, 7)
    first_key, second_key = jax.random.split(key)
    position = jnp.arange(NP, dtype=jnp.int32)
    row_index = position // (PD * N_COL)
    first = row_index * BR + jax.random.randint(first_key, (NP,), 0, BR, dtype=jnp.int32)
    first = jnp.minimum(first, NB - 2)
    span = NB - 1 - first
    offset = jax.random.randint(second_key, (NP,), 0, 1 << 20, dtype=jnp.int32) % span
    second = first + 1 + offset
    first = jnp.where(position == 0, 0, first)
    second = jnp.where(position == 0, NB - 1, second)
    return jnp.stack([first, second], axis=1).astype(jnp.int32)


def levels(rng, dims, cuts, smallest, top_value):
    gain, own = 1.0, jax.random.fold_in(rng, 6)
    for dim, blocks in cuts:
        draws = jnp.exp(jax.random.uniform(jax.random.fold_in(own, dim), (blocks,), jnp.float32, smallest / len(cuts), top_value / len(cuts)))
        gain = gain * jnp.repeat(draws, dims[dim] // blocks).reshape([-1 if axis == dim else 1 for axis in range(len(dims))])
    return gain


def gaussian(key, shape, deviation, reach, pieces=(), held_as=jnp.bfloat16):
    gain = levels(key, shape, pieces, -0.22, 0.18) if pieces else 1.0
    array = jax.random.normal(key, shape, jnp.float32) * deviation * gain
    return jnp.minimum(jnp.maximum(array, -reach), reach).astype(held_as)


def setup_inputs(seed: int = 0, part: int = 0) -> dict:
    key_of = jax.random.split(jax.random.key(seed), 6)
    part_splits = jax.random.split(jax.random.fold_in(key_of[5], part), 6)
    return {
        "tensor_tiles": gaussian(part_splits[0], (NP, 3, BLOCK, 3, BLOCK), (96 * BLOCK * PD * N_COL // BR) ** -0.5, 0.02734375, ((0, 16),)),
        "pair_blocks": draw_pair_blocks(jax.random.fold_in(jax.random.fold_in(key_of[5], part), 71), part),
        "polarizability": jnp.clip(jnp.exp(math.log(1.2) - 1.3862944 * jax.random.uniform(key_of[2], (NA,), jnp.float32) ** levels(key_of[2], (NA,), ((0, 4),), -0.2, 0.2)), 0.3, 1.2),
        "direct_field": gaussian(part_splits[3], (3, NA), 1.0, 6.0, ((1, 4),), jnp.float32),
        "cotangent": gaussian(part_splits[4], (3, NA), 1.0, 6.0, ((1, 4),), jnp.float32),
    }


def operate(tensor_tiles, pair_blocks, values):
    blocks = values.reshape(3, NB, BLOCK)
    groups = tensor_tiles.reshape(N_ROW, NP // N_ROW, 3, BLOCK, 3, BLOCK)
    pair_groups = pair_blocks.reshape(N_ROW, NP // N_ROW, 2)

    def step(total, item):
        tile, pairs = item
        tile = tile.astype(jnp.float32)
        near_side = blocks[:, pairs[:, 0]]
        far_side = blocks[:, pairs[:, 1]]
        row_part = jnp.einsum('paibj,bpj->api', tile, far_side, precision=lax.Precision.HIGHEST)
        col_part = jnp.einsum('paibj,api->bpj', tile, near_side, precision=lax.Precision.HIGHEST)
        total = total.at[:, pairs[:, 0]].add(row_part)
        total = total.at[:, pairs[:, 1]].add(col_part)
        return total, None

    total, unused = lax.scan(step, jnp.zeros((3, NB, BLOCK), jnp.float32), (groups, pair_groups))
    return total.reshape(3, NA)


def reference(tensor_tiles, pair_blocks, polarizability, direct_field, cotangent):
    mu_now = polarizability * direct_field
    rounded_mu = []
    for index in range(ITERS):
        rounded = mu_now.astype(jnp.bfloat16)
        rounded_mu.append(rounded.astype(jnp.float32))
        mu_now = polarizability * (direct_field + operate(tensor_tiles, pair_blocks, rounded_mu[-1]))
    dipoles = mu_now
    adjoint = cotangent
    rounded_w = [None] * ITERS
    field_grad = jnp.zeros_like(direct_field)
    for index in reversed(range(ITERS)):
        weighted = polarizability * adjoint
        field_grad = field_grad + weighted
        rounded_w[index] = weighted.astype(jnp.bfloat16).astype(jnp.float32)
        adjoint = operate(tensor_tiles, pair_blocks, rounded_w[index])
    field_grad = field_grad + polarizability * adjoint
    lefts = jnp.stack(rounded_w + rounded_mu).reshape(2 * ITERS, 3, NB, BLOCK)
    rights = jnp.stack(rounded_mu + rounded_w).reshape(2 * ITERS, 3, NB, BLOCK)

    def one_group(pairs):
        left_rows = lefts[:, :, pairs[:, 0]]
        right_rows = rights[:, :, pairs[:, 1]]
        outer = jnp.einsum('kapi,kbpj->paibj', left_rows, right_rows, precision=lax.Precision.HIGHEST)
        return outer.astype(jnp.bfloat16)

    tile_grad = lax.map(one_group, pair_blocks.reshape(N_ROW, NP // N_ROW, 2))
    tile_grad = tile_grad.reshape(NP, 3, BLOCK, 3, BLOCK)
    return dipoles, field_grad, tile_grad
```

```python
import functools

import jax
import jax.numpy as jnp
from jax import lax
from jax.experimental import pallas as pl
from jax.experimental.pallas import tpu as pltpu
from jax.sharding import PartitionSpec as P

ITERS = 3
MESH = pl.DeviceIdType.MESH
UNROLL_LIMIT = 32


def repeat(count, step):
    if count <= UNROLL_LIMIT:
        for index in range(count):
            step(index)
    else:
        lax.fori_loop(0, count, lambda index, carry: (step(index), carry)[1], 0)


def kernel(
    n_row,
    n_col,
    tiles_hbm,
    pairs,
    pol,
    field_in,
    cot_in,
    dip_out,
    grad_out,
    tg_hbm,
    tiles,
    tg,
    source,
    start_send,
    ag_send,
    ag_recv,
    rs_send,
    rs_recv,
    last_send,
    last_recv,
    fields,
    part,
    tile_sem,
    tg_sem,
    ag_send_sem,
    ag_recv_sem,
    rs_send_sem,
    rs_recv_sem,
    last_send_sem,
    last_recv_sem,
):
    group = n_row * n_col
    pair_count = tiles.shape[0]
    block = tiles.shape[3]
    local_blocks = pol.shape[0]
    owned = local_blocks // n_col
    chunk = rs_send.shape[2]
    row = lax.axis_index("row")
    col = lax.axis_index("col")
    me = row * n_col + col

    def peer_of(offset):
        return lax.rem(me + offset, group)

    def place(device):
        return {"row": device // n_col, "col": lax.rem(device, n_col)}

    for p in range(pair_count):
        pltpu.make_async_copy(tiles_hbm.at[p], tiles.at[p], tile_sem.at[p]).start()

    barrier = pltpu.get_barrier_semaphore()

    def greet(index):
        pl.semaphore_signal(
            barrier, inc=1, device_id=place(peer_of(index + 1)), device_id_type=MESH
        )

    repeat(group - 1, greet)

    even = lax.rem(lax.broadcasted_iota(jnp.int32, (8, block), 0), 2) == 0
    start_send[...] = jnp.zeros_like(start_send)
    part[...] = jnp.zeros_like(part)
    for b in range(local_blocks):
        lanes = pl.ds(b * block, block)
        source[b, 6:8, :] = jnp.zeros((2, block), jnp.float32)
        for c in range(3):
            source[b, 2 * c : 2 * c + 1, :] = field_in[c : c + 1, lanes]
            source[b, 2 * c + 1 : 2 * c + 2, :] = cot_in[c : c + 1, lanes]
    for o in range(n_col):
        rows = [pol[b : b + 1, :] * source[b] for b in range(o * owned, (o + 1) * owned)]
        rows += [jnp.zeros((8, block), jnp.float32)] * (chunk // 8 - owned)
        start_send[o] = jnp.concatenate(rows, axis=0).astype(jnp.bfloat16)

    pl.semaphore_wait(barrier, group - 1)

    def start_copy(index):
        other = lax.rem(row + index + 1, n_row)
        return pltpu.make_async_remote_copy(
            src_ref=start_send,
            dst_ref=ag_recv.at[0, pl.ds(row * n_col, n_col)],
            send_sem=ag_send_sem.at[0],
            recv_sem=ag_recv_sem.at[0],
            device_id={"row": other},
            device_id_type=MESH,
        )

    repeat(n_row - 1, lambda index: start_copy(index).start())
    ag_recv[0, pl.ds(row * n_col, n_col)] = start_send[...]

    def wait_for(ref, semaphore):
        pltpu.make_async_copy(ref, ref, semaphore).wait()

    mine = [source[col * owned + i] for i in range(owned)]
    pols = [pol[pl.ds(col * owned + i, 1), :] for i in range(owned)]
    now = [pols[i] * mine[i] for i in range(owned)]
    total = list(now)
    constant = [jnp.where(even, mine[i], 0.0) for i in range(owned)]
    first = [pairs[0, p] for p in range(pair_count)]
    second = [pairs[1, p] for p in range(pair_count)]

    def vector(step, at):
        return jnp.concatenate(
            [fields[step, at, 2 * c : 2 * c + 2, :] for c in range(3)], axis=1
        )

    for step in range(ITERS):
        if step == 0:
            wait_for(ag_recv.at[0, pl.ds(0, (n_row - 1) * n_col)], ag_recv_sem.at[0])
        else:
            wait_for(ag_recv.at[step, pl.ds(0, group - 1)], ag_recv_sem.at[step])

        def unpack(index):
            got = ag_recv[step, index].astype(jnp.float32)
            for i in range(owned):
                fields[step, index * owned + i] = got[8 * i : 8 * i + 8]

        repeat(group, unpack)

        for p in range(pair_count):
            if step == 0:
                pltpu.make_async_copy(tiles_hbm.at[p], tiles.at[p], tile_sem.at[p]).wait()
            near = vector(step, first[p]).astype(jnp.bfloat16)
            far = vector(step, second[p]).astype(jnp.bfloat16)
            tile = jnp.concatenate(
                [
                    jnp.concatenate([tiles[p, a, b] for b in range(3)], axis=1)
                    for a in range(3)
                ],
                axis=0,
            )
            to_second = lax.dot_general(
                near, tile, (((1,), (0,)), ((), ())), preferred_element_type=jnp.float32
            )
            to_first = lax.dot_general(
                far, tile, (((1,), (1,)), ((), ())), preferred_element_type=jnp.float32
            )
            for c in range(3):
                lanes = slice(c * block, (c + 1) * block)
                part[p, 2 * c : 2 * c + 2, :] = to_first[:, lanes]
                part[pair_count + p, 2 * c : 2 * c + 2, :] = to_second[:, lanes]

        terms = [part[i] for i in range(2 * pair_count)]
        ids = [jnp.full((8, block), at, jnp.int32) for at in first + second]

        def gathered(owner):
            sums = []
            for i in range(owned):
                at = owner * owned + i
                got = jnp.zeros((8, block), jnp.float32)
                for term, which in zip(terms, ids):
                    got = got + jnp.where(which == at, term, 0.0)
                sums.append(got)
            return sums

        def send_part(index):
            peer = peer_of(index + 1)
            rows = gathered(peer)
            rows += [jnp.zeros((8, block), jnp.float32)] * (chunk // 8 - owned)
            rs_send[step, peer] = jnp.concatenate(rows, axis=0).astype(jnp.bfloat16)
            pltpu.make_async_remote_copy(
                src_ref=rs_send.at[step, peer],
                dst_ref=rs_recv.at[step, me],
                send_sem=rs_send_sem.at[step],
                recv_sem=rs_recv_sem.at[step],
                device_id=place(peer),
                device_id_type=MESH,
            ).start()

        repeat(group - 1, send_part)
        own = gathered(me)
        rs_recv[step, me] = jnp.zeros((chunk, block), jnp.bfloat16)

        if step == ITERS - 1:
            for p in range(pair_count):
                left, right = [], []
                for t in range(ITERS):
                    left.append(vector(t, first[p]))
                    other = vector(ITERS - 1 - t, second[p])
                    right += [other[1:2], other[0:1]]
                blank = jnp.zeros((2, 3 * block), jnp.float32)
                left = jnp.concatenate(left + [blank], axis=0)
                right = jnp.concatenate(right + [blank], axis=0).astype(jnp.bfloat16)
                for a in range(3):
                    piece = left[:, a * block : (a + 1) * block].T.astype(jnp.bfloat16)
                    outer = jnp.dot(piece, right, preferred_element_type=jnp.float32)
                    for b in range(3):
                        tg[p, a, b] = outer[:, b * block : (b + 1) * block].astype(jnp.bfloat16)
                pltpu.make_async_copy(tg.at[p], tg_hbm.at[p], tg_sem.at[p]).start()

        wait_for(rs_recv.at[step, pl.ds(0, group - 1)], rs_recv_sem.at[step])

        def add(index, sums):
            got = rs_recv[step, index].astype(jnp.float32)
            return tuple(sums[i] + got[8 * i : 8 * i + 8] for i in range(owned))

        if group <= UNROLL_LIMIT:
            sums = tuple(own)
            for index in range(group):
                sums = add(index, sums)
        else:
            sums = lax.fori_loop(0, group, add, tuple(own))
        now = [pols[i] * (constant[i] + sums[i]) for i in range(owned)]
        total = [total[i] + now[i] for i in range(owned)]

        if step < ITERS - 1:
            rows = list(now) + [jnp.zeros((8, block), jnp.float32)] * (chunk // 8 - owned)
            packed = jnp.concatenate(rows, axis=0).astype(jnp.bfloat16)
            ag_send[step] = packed

            def send_field(index):
                pltpu.make_async_remote_copy(
                    src_ref=ag_send.at[step],
                    dst_ref=ag_recv.at[step + 1, me],
                    send_sem=ag_send_sem.at[step + 1],
                    recv_sem=ag_recv_sem.at[step + 1],
                    device_id=place(peer_of(index + 1)),
                    device_id_type=MESH,
                ).start()

            repeat(group - 1, send_field)
            ag_recv[step + 1, me] = packed

    for i in range(owned):
        last_send[i] = jnp.where(even, now[i], total[i])

    def last_copy(index):
        return pltpu.make_async_remote_copy(
            src_ref=last_send,
            dst_ref=last_recv.at[col],
            send_sem=last_send_sem,
            recv_sem=last_recv_sem,
            device_id={"col": lax.rem(col + index + 1, n_col)},
            device_id_type=MESH,
        )

    repeat(n_col - 1, lambda index: last_copy(index).start())
    last_recv[col] = last_send[...]
    wait_for(last_recv.at[pl.ds(0, n_col - 1)], last_recv_sem)
    for b in range(local_blocks):
        lanes = pl.ds(b * block, block)
        for c in range(3):
            dip_out[c : c + 1, lanes] = last_recv[b // owned, b % owned, 2 * c : 2 * c + 1, :]
            grad_out[c : c + 1, lanes] = last_recv[b // owned, b % owned, 2 * c + 1 : 2 * c + 2, :]

    wait_for(ag_recv.at[0, pl.ds(0, (n_row - 1) * n_col)], ag_send_sem.at[0])
    for step in range(ITERS):
        wait_for(rs_send.at[step, pl.ds(0, group - 1)], rs_send_sem.at[step])
        if step > 0:
            wait_for(ag_recv.at[step, pl.ds(0, group - 1)], ag_send_sem.at[step])
    wait_for(last_recv.at[pl.ds(0, n_col - 1)], last_send_sem)
    for p in range(pair_count):
        pltpu.make_async_copy(tg.at[p], tg_hbm.at[p], tg_sem.at[p]).wait()


def per_device(tensor_tiles, pair_blocks, polarizability, direct_field, cotangent):
    n_row = lax.axis_size("row")
    n_col = lax.axis_size("col")
    group = n_row * n_col
    pair_count = tensor_tiles.shape[0]
    block = tensor_tiles.shape[2]
    local_blocks = polarizability.shape[0] // block
    owned = local_blocks // n_col
    chunk = max(16, 8 * owned)
    f32, bf16 = jnp.float32, jnp.bfloat16
    tiles = tensor_tiles.transpose(0, 1, 3, 2, 4)
    vmem = pl.BlockSpec(memory_space=pltpu.VMEM)
    anywhere = pl.BlockSpec(memory_space=pl.ANY)
    dma = pltpu.SemaphoreType.DMA
    dipoles, grad, tile_grad = pl.pallas_call(
        functools.partial(kernel, n_row, n_col),
        out_shape=(
            jax.ShapeDtypeStruct(direct_field.shape, f32),
            jax.ShapeDtypeStruct(direct_field.shape, f32),
            jax.ShapeDtypeStruct(tiles.shape, bf16),
        ),
        in_specs=[anywhere, pl.BlockSpec(memory_space=pltpu.SMEM), vmem, vmem, vmem],
        out_specs=(vmem, vmem, anywhere),
        scratch_shapes=[
            pltpu.VMEM(tiles.shape, bf16),
            pltpu.VMEM(tiles.shape, bf16),
            pltpu.VMEM((local_blocks, 8, block), f32),
            pltpu.VMEM((n_col, chunk, block), bf16),
            pltpu.VMEM((ITERS - 1, chunk, block), bf16),
            pltpu.VMEM((ITERS, group, chunk, block), bf16),
            pltpu.VMEM((ITERS, group, chunk, block), bf16),
            pltpu.VMEM((ITERS, group, chunk, block), bf16),
            pltpu.VMEM((owned, 8, block), f32),
            pltpu.VMEM((n_col, owned, 8, block), f32),
            pltpu.VMEM((ITERS, group * owned, 8, block), f32),
            pltpu.VMEM((2 * pair_count, 8, block), f32),
            dma((pair_count,)),
            dma((pair_count,)),
            dma((ITERS,)),
            dma((ITERS,)),
            dma((ITERS,)),
            dma((ITERS,)),
            dma,
            dma,
        ],
        compiler_params=pltpu.CompilerParams(
            collective_id=0, has_side_effects=True, vmem_limit_bytes=32 * 1024 * 1024
        ),
    )(
        tiles,
        pair_blocks.T,
        polarizability.reshape(local_blocks, block),
        direct_field,
        cotangent,
    )
    return dipoles, grad, tile_grad.transpose(0, 1, 3, 2, 4)


def solution(mesh):
    placed = (
        P(("bead", "row", "col"), None, None, None, None),
        P(("bead", "row", "col"), None),
        P("row"),
        P(None, ("bead", "row")),
        P(None, ("bead", "row")),
    )
    return jax.shard_map(
        per_device,
        mesh=mesh,
        in_specs=placed,
        out_specs=(
            P(None, ("bead", "row")),
            P(None, ("bead", "row")),
            P(("bead", "row", "col"), None, None, None, None),
        ),
        check_vma=False,
    )
```

```python
import functools

import jax
import jax.numpy as jnp
from jax import lax
from jax.experimental import pallas as pl
from jax.experimental.pallas import tpu as pltpu
from jax.sharding import PartitionSpec as P

ITERS = 3
MESH = pl.DeviceIdType.MESH
UNROLL_LIMIT = 32


def repeat(count, step):
    if count <= UNROLL_LIMIT:
        for index in range(count):
            step(index)
    else:
        lax.fori_loop(0, count, lambda index, carry: (step(index), carry)[1], 0)


def loop(start, end, step):
    lax.fori_loop(start, end, lambda index, carry: (step(index), carry)[1], 0)


def kernel(
    n_row,
    n_col,
    tiles_hbm,
    pairs_hbm,
    pol_hbm,
    field_hbm,
    cot_hbm,
    dip_out,
    grad_out,
    tg_out,
    tiles,
    tg,
    dip,
    grad,
    pairs,
    pol,
    field_in,
    cot_in,
    stage,
    ag_send,
    ag_recv,
    rs_send,
    rs_recv,
    fields,
    part,
    tile_sem,
    tg_sem,
    in_sem,
    out_sem,
    ag_send_sem,
    ag_recv_sem,
    rs_send_sem,
    rs_recv_sem,
):
    group = n_row * n_col
    pair_count = tiles.shape[0]
    block = tiles.shape[3]
    local_blocks = pol.shape[0]
    chunk = ag_send.shape[1]
    row = lax.axis_index("row")
    col = lax.axis_index("col")
    me = row * n_col + col

    inputs = [
        pltpu.make_async_copy(source, target, in_sem.at[index])
        for index, (source, target) in enumerate(
            ((pairs_hbm, pairs), (pol_hbm, pol), (field_hbm, field_in), (cot_hbm, cot_in))
        )
    ]
    tile_copies = [
        pltpu.make_async_copy(tiles_hbm.at[p], tiles.at[p], tile_sem.at[p])
        for p in range(pair_count)
    ]
    barrier = pltpu.get_barrier_semaphore()

    def greet(index):
        peer = lax.rem(me + index + 1, group)
        pl.semaphore_signal(
            barrier,
            inc=1,
            device_id={"row": peer // n_col, "col": lax.rem(peer, n_col)},
            device_id_type=MESH,
        )

    repeat(group - 1, greet)
    for copy in inputs + tile_copies:
        copy.start()
    for copy in inputs:
        copy.wait()

    index = lax.broadcasted_iota(jnp.int32, (chunk, block), 0)
    even = lax.rem(index, 2) == 0
    stage[...] = jnp.zeros_like(stage)
    part[...] = jnp.zeros_like(part)
    for b in range(local_blocks):
        lanes = pl.ds(b * block, block)
        for c in range(3):
            at = 6 * b + 2 * c
            stage[0, at : at + 1, :] = field_in[c : c + 1, lanes]
            stage[0, at + 1 : at + 2, :] = cot_in[c : c + 1, lanes]
        stage[1, 6 * b : 6 * b + 6, :] = jnp.broadcast_to(pol[b : b + 1, :], (6, block))
    source = stage[0]
    pols = stage[1]
    now = pols * source
    total = now
    constant = jnp.where(even, source, 0.0)
    first = [pairs[0, p] for p in range(pair_count)]
    second = [pairs[1, p] for p in range(pair_count)]
    first_ids = [jnp.full((8, block), at, jnp.int32) for at in first]
    second_ids = [jnp.full((8, block), at, jnp.int32) for at in second]

    def wait_for(ref, semaphore):
        pltpu.make_async_copy(ref, ref, semaphore).wait()

    def vector(step, at):
        return jnp.concatenate(
            [fields[step, at, 2 * c : 2 * c + 2, :] for c in range(3)], axis=1
        )

    def unpack(step, which_row, packed):
        stage[2] = packed.astype(jnp.float32)
        for b in range(local_blocks):
            fields[step, which_row * local_blocks + b, 0:6, :] = stage[2, 6 * b : 6 * b + 6, :]

    def matrix(p):
        return jnp.concatenate(
            [
                jnp.concatenate([tiles[p, a, b] for b in range(3)], axis=1)
                for a in range(3)
            ],
            axis=0,
        )

    def keep(slot, values):
        for c in range(3):
            part[slot, 2 * c : 2 * c + 2, :] = values[:, c * block : (c + 1) * block]

    def summed(which_row, slots, ids):
        terms = [part[slot] for slot in slots]
        for b in range(local_blocks):
            at = which_row * local_blocks + b
            got = jnp.where(ids[0] == at, terms[0], 0.0)
            for term, which in zip(terms[1:], ids[1:]):
                got = got + jnp.where(which == at, term, 0.0)
            stage[3, 6 * b : 6 * b + 6, :] = got[0:6]
        return stage[3].astype(jnp.bfloat16)

    def part_copy(step, target_row, target_col):
        return pltpu.make_async_remote_copy(
            src_ref=rs_send.at[step, target_row],
            dst_ref=rs_recv.at[step, row, col],
            send_sem=rs_send_sem.at[step, target_row],
            recv_sem=rs_recv_sem.at[step, row],
            device_id={"row": target_row, "col": target_col},
            device_id_type=MESH,
        )

    pl.semaphore_wait(barrier, group - 1)

    for step in range(ITERS):
        packed = now.astype(jnp.bfloat16)
        ag_send[step] = packed

        def send_field(index):
            pltpu.make_async_remote_copy(
                src_ref=ag_send.at[step],
                dst_ref=ag_recv.at[step, row],
                send_sem=ag_send_sem.at[step],
                recv_sem=ag_recv_sem.at[step],
                device_id={"row": lax.rem(row + index + 1, n_row)},
                device_id_type=MESH,
            ).start()

        repeat(n_row - 1, send_field)
        ag_recv[step, row] = packed
        unpack(step, row, packed)

        for p in range(pair_count):
            if step == 0:
                tile_copies[p].wait()
            near = vector(step, first[p]).astype(jnp.bfloat16)
            keep(
                pair_count + p,
                lax.dot_general(
                    near,
                    matrix(p),
                    (((1,), (0,)), ((), ())),
                    preferred_element_type=jnp.float32,
                ),
            )

        def send_later(back):
            target = n_row - 1 - back
            rs_send[step, target] = summed(
                target, range(pair_count, 2 * pair_count), second_ids
            )
            for k in range(n_col):
                part_copy(step, target, lax.rem(col + k, n_col)).start()

        loop(0, n_row - 1 - row, send_later)

        wait_for(ag_recv.at[step, pl.ds(0, n_row - 1)], ag_recv_sem.at[step])
        repeat(n_row, lambda index: unpack(step, index, ag_recv[step, index]))
        for p in range(pair_count):
            far = vector(step, second[p]).astype(jnp.bfloat16)
            keep(
                p,
                lax.dot_general(
                    far,
                    matrix(p),
                    (((1,), (1,)), ((), ())),
                    preferred_element_type=jnp.float32,
                ),
            )
        own = summed(row, range(2 * pair_count), first_ids + second_ids)
        rs_send[step, row] = own
        for k in range(1, n_col):
            part_copy(step, row, lax.rem(col + k, n_col)).start()
        rs_recv[step, row, col] = own

        if step == ITERS - 1:
            for p in range(pair_count):
                left, right = [], []
                for t in range(ITERS):
                    left.append(vector(t, first[p]))
                    other = vector(ITERS - 1 - t, second[p])
                    right += [other[1:2], other[0:1]]
                blank = jnp.zeros((2, 3 * block), jnp.float32)
                left = jnp.concatenate(left + [blank], axis=0)
                right = jnp.concatenate(right + [blank], axis=0).astype(jnp.bfloat16)
                for a in range(3):
                    piece = left[:, a * block : (a + 1) * block].T.astype(jnp.bfloat16)
                    outer = jnp.dot(piece, right, preferred_element_type=jnp.float32)
                    for b in range(3):
                        tg[p, a, b] = outer[:, b * block : (b + 1) * block].astype(jnp.bfloat16)
                pltpu.make_async_copy(tg.at[p], tg_out.at[p], tg_sem.at[p]).start()

        def add_row(source_row, sums):
            for c in range(n_col):
                sums = sums + rs_recv[step, source_row, c].astype(jnp.float32)
            return sums

        def take(source_row, sums):
            wait_for(
                rs_recv.at[step, 0, pl.ds(0, n_col)], rs_recv_sem.at[step, source_row]
            )
            return add_row(source_row, sums)

        sums = lax.fori_loop(0, row, take, jnp.zeros((chunk, block), jnp.float32))
        wait_for(rs_recv.at[step, 0, pl.ds(0, n_col - 1)], rs_recv_sem.at[step, row])
        now = pols * (constant + add_row(row, sums))
        total = total + now

    stage[2] = now
    stage[3] = total
    for b in range(local_blocks):
        lanes = pl.ds(b * block, block)
        for c in range(3):
            at = 6 * b + 2 * c
            dip[c : c + 1, lanes] = stage[2, at : at + 1, :]
            grad[c : c + 1, lanes] = stage[3, at + 1 : at + 2, :]
    results = [
        pltpu.make_async_copy(dip, dip_out, out_sem.at[0]),
        pltpu.make_async_copy(grad, grad_out, out_sem.at[1]),
    ]
    for copy in results:
        copy.start()

    for step in range(ITERS):
        wait_for(ag_recv.at[step, pl.ds(0, n_row - 1)], ag_send_sem.at[step])
        wait_for(rs_recv.at[step, 0, pl.ds(0, n_col - 1)], rs_send_sem.at[step, row])
        loop(
            row + 1,
            n_row,
            lambda target: wait_for(
                rs_recv.at[step, 0, pl.ds(0, n_col)], rs_send_sem.at[step, target]
            ),
        )
    for p in range(pair_count):
        pltpu.make_async_copy(tg.at[p], tg_out.at[p], tg_sem.at[p]).wait()
    for copy in results:
        copy.wait()


def copy_out(dip, grad, tg, dip_out, grad_out, tg_out, dip_held, grad_held, tg_held, sems):
    pieces = [(tg.at[p], tg_held.at[p], tg_out.at[p]) for p in range(tg.shape[0])]
    pieces += [(dip, dip_held, dip_out), (grad, grad_held, grad_out)]
    loads = [
        pltpu.make_async_copy(source, held, sems.at[0, i])
        for i, (source, held, _) in enumerate(pieces)
    ]
    stores = [
        pltpu.make_async_copy(held, target, sems.at[1, i])
        for i, (_, held, target) in enumerate(pieces)
    ]
    for load in loads:
        load.start()
    for load, store in zip(loads, stores):
        load.wait()
        store.start()
    for store in stores:
        store.wait()


def per_device(tensor_tiles, pair_blocks, polarizability, direct_field, cotangent):
    n_row = lax.axis_size("row")
    n_col = lax.axis_size("col")
    pair_count = tensor_tiles.shape[0]
    block = tensor_tiles.shape[2]
    local_blocks = polarizability.shape[0] // block
    chunk = -(-6 * local_blocks // 16) * 16
    f32, bf16 = jnp.float32, jnp.bfloat16
    tiles = tensor_tiles.transpose(0, 1, 3, 2, 4)
    hbm = pl.BlockSpec(memory_space=pltpu.HBM)
    anywhere = pl.BlockSpec(memory_space=pl.ANY)
    dma = pltpu.SemaphoreType.DMA
    shapes = (
        jax.ShapeDtypeStruct(direct_field.shape, f32),
        jax.ShapeDtypeStruct(direct_field.shape, f32),
        jax.ShapeDtypeStruct(tiles.shape, bf16),
    )
    results = pl.pallas_call(
        functools.partial(kernel, n_row, n_col),
        out_shape=shapes,
        in_specs=[hbm] * 5,
        out_specs=(anywhere,) * 3,
        scratch_shapes=[
            pltpu.VMEM(tiles.shape, bf16),
            pltpu.VMEM(tiles.shape, bf16),
            pltpu.VMEM(direct_field.shape, f32),
            pltpu.VMEM(direct_field.shape, f32),
            pltpu.SMEM((2, pair_count), jnp.int32),
            pltpu.VMEM((local_blocks, block), f32),
            pltpu.VMEM(direct_field.shape, f32),
            pltpu.VMEM(direct_field.shape, f32),
            pltpu.VMEM((4, chunk, block), f32),
            pltpu.VMEM((ITERS, chunk, block), bf16),
            pltpu.VMEM((ITERS, n_row, chunk, block), bf16),
            pltpu.VMEM((ITERS, n_row, chunk, block), bf16),
            pltpu.VMEM((ITERS, n_row, n_col, chunk, block), bf16),
            pltpu.VMEM((ITERS, n_row * local_blocks, 8, block), f32),
            pltpu.VMEM((2 * pair_count, 8, block), f32),
            dma((pair_count,)),
            dma((pair_count,)),
            dma((4,)),
            dma((2,)),
            dma((ITERS,)),
            dma((ITERS,)),
            dma((ITERS, n_row)),
            dma((ITERS, n_row)),
        ],
        compiler_params=pltpu.CompilerParams(
            collective_id=0, has_side_effects=True, vmem_limit_bytes=60 * 1024 * 1024
        ),
    )(
        tiles,
        pair_blocks.T,
        polarizability.reshape(local_blocks, block),
        direct_field,
        cotangent,
    )
    dipoles, grad, tile_grad = pl.pallas_call(
        copy_out,
        out_shape=shapes,
        in_specs=[anywhere] * 3,
        out_specs=(anywhere,) * 3,
        scratch_shapes=[
            pltpu.VMEM(direct_field.shape, f32),
            pltpu.VMEM(direct_field.shape, f32),
            pltpu.VMEM(tiles.shape, bf16),
            dma((2, pair_count + 2)),
        ],
    )(*results)
    return dipoles, grad, tile_grad.transpose(0, 1, 3, 2, 4)


def solution(mesh):
    placed = (
        P(("bead", "row", "col"), None, None, None, None),
        P(("bead", "row", "col"), None),
        P("row"),
        P(None, ("bead", "row")),
        P(None, ("bead", "row")),
    )
    return jax.shard_map(
        per_device,
        mesh=mesh,
        in_specs=placed,
        out_specs=(
            P(None, ("bead", "row")),
            P(None, ("bead", "row")),
            P(("bead", "row", "col"), None, None, None, None),
        ),
        check_vma=False,
    )
```

```python
import functools

import jax
import jax.numpy as jnp
from jax import lax
from jax.experimental import pallas as pl
from jax.experimental.pallas import tpu as pltpu
from jax.sharding import PartitionSpec as P

ITERS = 3
MESH = pl.DeviceIdType.MESH
UNROLL_LIMIT = 32


def repeat(count, step):
    if count <= UNROLL_LIMIT:
        for index in range(count):
            step(index)
    else:
        lax.fori_loop(0, count, lambda index, carry: (step(index), carry)[1], 0)


def loop(start, end, step):
    lax.fori_loop(start, end, lambda index, carry: (step(index), carry)[1], 0)


def kernel(
    n_row,
    n_col,
    tiles_hbm,
    pairs_hbm,
    pol_hbm,
    field_hbm,
    cot_hbm,
    dip,
    grad,
    tg,
    tiles,
    pairs,
    pol,
    field_in,
    cot_in,
    stage,
    ag_send,
    ag_recv,
    rs_send,
    rs_recv,
    fields,
    part,
    tile_sem,
    in_sem,
    ag_send_sem,
    ag_recv_sem,
    rs_send_sem,
    rs_recv_sem,
):
    group = n_row * n_col
    pair_count = tiles.shape[0]
    block = tiles.shape[3]
    local_blocks = pol.shape[0]
    chunk = ag_send.shape[1]
    row = lax.axis_index("row")
    col = lax.axis_index("col")
    me = row * n_col + col

    inputs = [
        pltpu.make_async_copy(source, target, in_sem.at[index])
        for index, (source, target) in enumerate(
            ((pairs_hbm, pairs), (pol_hbm, pol), (field_hbm, field_in), (cot_hbm, cot_in))
        )
    ]
    tile_copies = [
        pltpu.make_async_copy(tiles_hbm.at[p], tiles.at[p], tile_sem.at[p])
        for p in range(pair_count)
    ]
    barrier = pltpu.get_barrier_semaphore()

    def greet(index):
        peer = lax.rem(me + index + 1, group)
        pl.semaphore_signal(
            barrier,
            inc=1,
            device_id={"row": peer // n_col, "col": lax.rem(peer, n_col)},
            device_id_type=MESH,
        )

    repeat(group - 1, greet)
    for copy in inputs + tile_copies:
        copy.start()
    for copy in inputs:
        copy.wait()

    index = lax.broadcasted_iota(jnp.int32, (chunk, block), 0)
    even = lax.rem(index, 2) == 0
    stage[...] = jnp.zeros_like(stage)
    part[...] = jnp.zeros_like(part)
    for b in range(local_blocks):
        lanes = pl.ds(b * block, block)
        for c in range(3):
            at = 6 * b + 2 * c
            stage[0, at : at + 1, :] = field_in[c : c + 1, lanes]
            stage[0, at + 1 : at + 2, :] = cot_in[c : c + 1, lanes]
        stage[1, 6 * b : 6 * b + 6, :] = jnp.broadcast_to(pol[b : b + 1, :], (6, block))
    source = stage[0]
    pols = stage[1]
    now = pols * source
    total = now
    constant = jnp.where(even, source, 0.0)
    first = [pairs[0, p] for p in range(pair_count)]
    second = [pairs[1, p] for p in range(pair_count)]
    first_ids = [jnp.full((8, block), at, jnp.int32) for at in first]
    second_ids = [jnp.full((8, block), at, jnp.int32) for at in second]

    def wait_for(ref, semaphore):
        pltpu.make_async_copy(ref, ref, semaphore).wait()

    def vector(step, at):
        return jnp.concatenate(
            [fields[step, at, 2 * c : 2 * c + 2, :] for c in range(3)], axis=1
        )

    def unpack(step, which_row, packed):
        stage[2] = packed.astype(jnp.float32)
        for b in range(local_blocks):
            fields[step, which_row * local_blocks + b, 0:6, :] = stage[2, 6 * b : 6 * b + 6, :]

    def matrix(p):
        return jnp.concatenate(
            [
                jnp.concatenate([tiles[p, a, b] for b in range(3)], axis=1)
                for a in range(3)
            ],
            axis=0,
        )

    def keep(slot, values):
        for c in range(3):
            part[slot, 2 * c : 2 * c + 2, :] = values[:, c * block : (c + 1) * block]

    def summed(which_row, slots, ids):
        terms = [part[slot] for slot in slots]
        for b in range(local_blocks):
            at = which_row * local_blocks + b
            got = jnp.where(ids[0] == at, terms[0], 0.0)
            for term, which in zip(terms[1:], ids[1:]):
                got = got + jnp.where(which == at, term, 0.0)
            stage[3, 6 * b : 6 * b + 6, :] = got[0:6]
        return stage[3]

    def part_copy(step, target_row, target_col):
        return pltpu.make_async_remote_copy(
            src_ref=rs_send.at[step, target_row],
            dst_ref=rs_recv.at[step, row, col],
            send_sem=rs_send_sem.at[step, target_row],
            recv_sem=rs_recv_sem.at[step, row],
            device_id={"row": target_row, "col": target_col},
            device_id_type=MESH,
        )

    pl.semaphore_wait(barrier, group - 1)

    for step in range(ITERS):
        packed = now.astype(jnp.bfloat16)
        ag_send[step] = packed

        def send_field(target):
            pltpu.make_async_remote_copy(
                src_ref=ag_send.at[step],
                dst_ref=ag_recv.at[step, row],
                send_sem=ag_send_sem.at[step, target],
                recv_sem=ag_recv_sem.at[step, row],
                device_id={"row": target},
                device_id_type=MESH,
            ).start()

        loop(0, row, send_field)
        unpack(step, row, packed)

        for p in range(pair_count):
            if step == 0:
                tile_copies[p].wait()
            near = vector(step, first[p]).astype(jnp.bfloat16)
            keep(
                pair_count + p,
                lax.dot_general(
                    near,
                    matrix(p),
                    (((1,), (0,)), ((), ())),
                    preferred_element_type=jnp.float32,
                ),
            )

        def send_later(back):
            target = n_row - 1 - back
            later = summed(target, range(pair_count, 2 * pair_count), second_ids)
            rs_send[step, target] = later.astype(jnp.bfloat16)
            for k in range(n_col):
                part_copy(step, target, lax.rem(col + k, n_col)).start()

        loop(0, n_row - 1 - row, send_later)

        stage[4] = summed(row, range(pair_count, 2 * pair_count), second_ids)

        def take_field(source_row):
            wait_for(ag_send.at[step], ag_recv_sem.at[step, source_row])
            unpack(step, source_row, ag_recv[step, source_row])

        loop(row + 1, n_row, take_field)
        for p in range(pair_count):
            far = vector(step, second[p]).astype(jnp.bfloat16)
            keep(
                p,
                lax.dot_general(
                    far,
                    matrix(p),
                    (((1,), (1,)), ((), ())),
                    preferred_element_type=jnp.float32,
                ),
            )
        own = (stage[4] + summed(row, range(pair_count), first_ids)).astype(jnp.bfloat16)
        rs_send[step, row] = own
        for k in range(1, n_col):
            part_copy(step, row, lax.rem(col + k, n_col)).start()
        rs_recv[step, row, col] = own

        if step == ITERS - 1:
            for p in range(pair_count):
                left, right = [], []
                for t in range(ITERS):
                    left.append(vector(t, first[p]))
                    other = vector(ITERS - 1 - t, second[p])
                    right += [other[1:2], other[0:1]]
                blank = jnp.zeros((2, 3 * block), jnp.float32)
                left = jnp.concatenate(left + [blank], axis=0)
                right = jnp.concatenate(right + [blank], axis=0).astype(jnp.bfloat16)
                for a in range(3):
                    piece = left[:, a * block : (a + 1) * block].T.astype(jnp.bfloat16)
                    outer = jnp.dot(piece, right, preferred_element_type=jnp.float32)
                    for b in range(3):
                        tg[p, a, b] = outer[:, b * block : (b + 1) * block].astype(jnp.bfloat16)

        def add_row(source_row, sums):
            for c in range(n_col):
                sums = sums + rs_recv[step, source_row, c].astype(jnp.float32)
            return sums

        def take(source_row, sums):
            wait_for(
                rs_recv.at[step, 0, pl.ds(0, n_col)], rs_recv_sem.at[step, source_row]
            )
            return add_row(source_row, sums)

        sums = lax.fori_loop(0, row, take, jnp.zeros((chunk, block), jnp.float32))
        wait_for(rs_recv.at[step, 0, pl.ds(0, n_col - 1)], rs_recv_sem.at[step, row])
        now = pols * (constant + add_row(row, sums))
        total = total + now

    stage[2] = now
    stage[3] = total
    for b in range(local_blocks):
        lanes = pl.ds(b * block, block)
        for c in range(3):
            at = 6 * b + 2 * c
            dip[c : c + 1, lanes] = stage[2, at : at + 1, :]
            grad[c : c + 1, lanes] = stage[3, at + 1 : at + 2, :]

    for step in range(ITERS):
        loop(0, row, lambda target: wait_for(ag_send.at[step], ag_send_sem.at[step, target]))
        wait_for(rs_recv.at[step, 0, pl.ds(0, n_col - 1)], rs_send_sem.at[step, row])
        loop(
            row + 1,
            n_row,
            lambda target: wait_for(
                rs_recv.at[step, 0, pl.ds(0, n_col)], rs_send_sem.at[step, target]
            ),
        )


def copy_out(*refs):
    count = (len(refs) - 1) // 2
    copies = [
        pltpu.make_async_copy(refs[i], refs[count + i], refs[-1].at[i]) for i in range(count)
    ]
    for copy in copies[::-1]:
        copy.start()
    for copy in copies:
        copy.wait()


def per_device(tensor_tiles, pair_blocks, polarizability, direct_field, cotangent):
    n_row = lax.axis_size("row")
    n_col = lax.axis_size("col")
    pair_count = tensor_tiles.shape[0]
    block = tensor_tiles.shape[2]
    local_blocks = polarizability.shape[0] // block
    chunk = -(-6 * local_blocks // 16) * 16
    f32, bf16 = jnp.float32, jnp.bfloat16
    tiles = tensor_tiles.transpose(0, 1, 3, 2, 4)
    vmem = pl.BlockSpec(memory_space=pltpu.VMEM)
    hbm = pl.BlockSpec(memory_space=pltpu.HBM)
    anywhere = pl.BlockSpec(memory_space=pl.ANY)
    dma = pltpu.SemaphoreType.DMA
    shapes = (
        jax.ShapeDtypeStruct(direct_field.shape, f32),
        jax.ShapeDtypeStruct(direct_field.shape, f32),
        jax.ShapeDtypeStruct(tiles.shape, bf16),
    )
    results = pl.pallas_call(
        functools.partial(kernel, n_row, n_col),
        out_shape=tuple(pltpu.VMEM(x.shape, x.dtype) for x in shapes),
        in_specs=[hbm] * 5,
        out_specs=(vmem,) * 3,
        scratch_shapes=[
            pltpu.VMEM(tiles.shape, bf16),
            pltpu.SMEM((2, pair_count), jnp.int32),
            pltpu.VMEM((local_blocks, block), f32),
            pltpu.VMEM(direct_field.shape, f32),
            pltpu.VMEM(direct_field.shape, f32),
            pltpu.VMEM((5, chunk, block), f32),
            pltpu.VMEM((ITERS, chunk, block), bf16),
            pltpu.VMEM((ITERS, n_row, chunk, block), bf16),
            pltpu.VMEM((ITERS, n_row, chunk, block), bf16),
            pltpu.VMEM((ITERS, n_row, n_col, chunk, block), bf16),
            pltpu.VMEM((ITERS, n_row * local_blocks, 8, block), f32),
            pltpu.VMEM((2 * pair_count, 8, block), f32),
            dma((pair_count,)),
            dma((4,)),
            dma((ITERS, n_row)),
            dma((ITERS, n_row)),
            dma((ITERS, n_row)),
            dma((ITERS, n_row)),
        ],
        compiler_params=pltpu.CompilerParams(
            collective_id=0, has_side_effects=True, vmem_limit_bytes=60 * 1024 * 1024
        ),
    )(
        tiles,
        pair_blocks.T,
        polarizability.reshape(local_blocks, block),
        direct_field,
        cotangent,
    )
    dipoles, grad, tile_grad = pl.pallas_call(
        copy_out,
        out_shape=shapes,
        in_specs=[vmem] * 3,
        out_specs=(anywhere,) * 3,
        scratch_shapes=[dma((3,))],
        compiler_params=pltpu.CompilerParams(vmem_limit_bytes=32 * 1024 * 1024),
    )(*results)
    return dipoles, grad, tile_grad.transpose(0, 1, 3, 2, 4)


def solution(mesh):
    placed = (
        P(("bead", "row", "col"), None, None, None, None),
        P(("bead", "row", "col"), None),
        P("row"),
        P(None, ("bead", "row")),
        P(None, ("bead", "row")),
    )
    return jax.shard_map(
        per_device,
        mesh=mesh,
        in_specs=placed,
        out_specs=(
            P(None, ("bead", "row")),
            P(None, ("bead", "row")),
            P(("bead", "row", "col"), None, None, None, None),
        ),
        check_vma=False,
    )
```

```python
import functools

import jax
import jax.numpy as jnp
from jax import lax
from jax.experimental import pallas as pl
from jax.experimental.pallas import tpu as pltpu
from jax.sharding import PartitionSpec as P

ITERS = 3
MESH = pl.DeviceIdType.MESH
UNROLL_LIMIT = 32


def repeat(count, step):
    if count <= UNROLL_LIMIT:
        for index in range(count):
            step(index)
    else:
        lax.fori_loop(0, count, lambda index, carry: (step(index), carry)[1], 0)


def loop(start, end, step):
    lax.fori_loop(start, end, lambda index, carry: (step(index), carry)[1], 0)


def kernel(
    n_row,
    n_col,
    tiles_hbm,
    pairs_hbm,
    pol_hbm,
    field_hbm,
    cot_hbm,
    dip,
    grad,
    tg,
    tiles,
    pairs,
    pol,
    field_in,
    cot_in,
    stage,
    ag_send,
    ag_recv,
    rs_send,
    rs_recv,
    fields,
    part,
    tile_sem,
    in_sem,
    ag_send_sem,
    ag_recv_sem,
    rs_send_sem,
    rs_recv_sem,
):
    group = n_row * n_col
    pair_count = tiles.shape[0]
    block = tiles.shape[3]
    local_blocks = pol.shape[0]
    chunk = ag_send.shape[1]
    row = lax.axis_index("row")
    col = lax.axis_index("col")
    me = row * n_col + col

    inputs = [
        pltpu.make_async_copy(source, target, in_sem.at[index])
        for index, (source, target) in enumerate(
            ((pairs_hbm, pairs), (pol_hbm, pol), (field_hbm, field_in), (cot_hbm, cot_in))
        )
    ]
    tile_copies = [
        pltpu.make_async_copy(tiles_hbm.at[p], tiles.at[p], tile_sem.at[p])
        for p in range(pair_count)
    ]
    barrier = pltpu.get_barrier_semaphore()

    def far_first(index):
        return jnp.where(2 * col < n_col, n_col - 1 - index, index)

    def greet(index):
        other_row = lax.rem(row + n_row // 2 + index, n_row)
        for k in range(n_col):
            other_col = far_first(k)

            @pl.when((other_row != row) | (other_col != col))
            def _():
                pl.semaphore_signal(
                    barrier,
                    inc=1,
                    device_id={"row": other_row, "col": other_col},
                    device_id_type=MESH,
                )

    repeat(n_row, greet)
    for copy in inputs + tile_copies:
        copy.start()
    for copy in inputs:
        copy.wait()

    index = lax.broadcasted_iota(jnp.int32, (chunk, block), 0)
    even = lax.rem(index, 2) == 0
    stage[...] = jnp.zeros_like(stage)
    part[...] = jnp.zeros_like(part)
    for b in range(local_blocks):
        lanes = pl.ds(b * block, block)
        for c in range(3):
            at = 6 * b + 2 * c
            stage[0, at : at + 1, :] = field_in[c : c + 1, lanes]
            stage[0, at + 1 : at + 2, :] = cot_in[c : c + 1, lanes]
        stage[1, 6 * b : 6 * b + 6, :] = jnp.broadcast_to(pol[b : b + 1, :], (6, block))
    source = stage[0]
    pols = stage[1]
    now = pols * source
    total = now
    constant = jnp.where(even, source, 0.0)
    first = [pairs[0, p] for p in range(pair_count)]
    second = [pairs[1, p] for p in range(pair_count)]
    first_ids = [jnp.full((8, block), at, jnp.int32) for at in first]
    second_ids = [jnp.full((8, block), at, jnp.int32) for at in second]

    def wait_for(ref, semaphore):
        pltpu.make_async_copy(ref, ref, semaphore).wait()

    def vector(step, at):
        return jnp.concatenate(
            [fields[step, at, 2 * c : 2 * c + 2, :] for c in range(3)], axis=1
        )

    def unpack(step, which_row, packed):
        stage[2] = packed.astype(jnp.float32)
        for b in range(local_blocks):
            fields[step, which_row * local_blocks + b, 0:6, :] = stage[2, 6 * b : 6 * b + 6, :]

    def matrix(p):
        return jnp.concatenate(
            [
                jnp.concatenate([tiles[p, a, b] for b in range(3)], axis=1)
                for a in range(3)
            ],
            axis=0,
        )

    def keep(slot, values):
        for c in range(3):
            part[slot, 2 * c : 2 * c + 2, :] = values[:, c * block : (c + 1) * block]

    def summed(which_row, slots, ids):
        terms = [part[slot] for slot in slots]
        for b in range(local_blocks):
            at = which_row * local_blocks + b
            got = jnp.where(ids[0] == at, terms[0], 0.0)
            for term, which in zip(terms[1:], ids[1:]):
                got = got + jnp.where(which == at, term, 0.0)
            stage[3, 6 * b : 6 * b + 6, :] = got[0:6]
        return stage[3]

    def part_copy(step, target_row, target_col):
        return pltpu.make_async_remote_copy(
            src_ref=rs_send.at[step, target_row],
            dst_ref=rs_recv.at[step, row, col],
            send_sem=rs_send_sem.at[step, target_row],
            recv_sem=rs_recv_sem.at[step, row],
            device_id={"row": target_row, "col": target_col},
            device_id_type=MESH,
        )

    pl.semaphore_wait(barrier, group - 1)

    for step in range(ITERS):
        packed = now.astype(jnp.bfloat16)
        ag_send[step] = packed

        def send_field(target):
            pltpu.make_async_remote_copy(
                src_ref=ag_send.at[step],
                dst_ref=ag_recv.at[step, row],
                send_sem=ag_send_sem.at[step, target],
                recv_sem=ag_recv_sem.at[step, row],
                device_id={"row": target},
                device_id_type=MESH,
            ).start()

        loop(0, row, send_field)
        unpack(step, row, packed)

        for p in range(pair_count):
            if step == 0:
                tile_copies[p].wait()
            near = vector(step, first[p]).astype(jnp.bfloat16)
            keep(
                pair_count + p,
                lax.dot_general(
                    near,
                    matrix(p),
                    (((1,), (0,)), ((), ())),
                    preferred_element_type=jnp.float32,
                ),
            )

        def send_later(back):
            target = n_row - 1 - back
            later = summed(target, range(pair_count, 2 * pair_count), second_ids)
            rs_send[step, target] = later.astype(jnp.bfloat16)
            for k in range(n_col):
                part_copy(step, target, far_first(k)).start()

        loop(0, n_row - 1 - row, send_later)

        stage[4] = summed(row, range(pair_count, 2 * pair_count), second_ids)

        def take_field(source_row):
            wait_for(ag_send.at[step], ag_recv_sem.at[step, source_row])
            unpack(step, source_row, ag_recv[step, source_row])

        loop(row + 1, n_row, take_field)
        for p in range(pair_count):
            far = vector(step, second[p]).astype(jnp.bfloat16)
            keep(
                p,
                lax.dot_general(
                    far,
                    matrix(p),
                    (((1,), (1,)), ((), ())),
                    preferred_element_type=jnp.float32,
                ),
            )
        own = (stage[4] + summed(row, range(pair_count), first_ids)).astype(jnp.bfloat16)
        rs_send[step, row] = own
        for k in range(n_col):
            target_col = far_first(k)

            @pl.when(target_col != col)
            def _():
                part_copy(step, row, target_col).start()

        rs_recv[step, row, col] = own

        if step == ITERS - 1:
            for p in range(pair_count):
                left, right = [], []
                for t in range(ITERS):
                    left.append(vector(t, first[p]))
                    other = vector(ITERS - 1 - t, second[p])
                    right += [other[1:2], other[0:1]]
                blank = jnp.zeros((2, 3 * block), jnp.float32)
                left = jnp.concatenate(left + [blank], axis=0)
                right = jnp.concatenate(right + [blank], axis=0).astype(jnp.bfloat16)
                for a in range(3):
                    piece = left[:, a * block : (a + 1) * block].T.astype(jnp.bfloat16)
                    outer = jnp.dot(piece, right, preferred_element_type=jnp.float32)
                    for b in range(3):
                        tg[p, a, b] = outer[:, b * block : (b + 1) * block].astype(jnp.bfloat16)

        def add_row(source_row, sums):
            for c in range(n_col):
                sums = sums + rs_recv[step, source_row, c].astype(jnp.float32)
            return sums

        def take(source_row, sums):
            wait_for(
                rs_recv.at[step, 0, pl.ds(0, n_col)], rs_recv_sem.at[step, source_row]
            )
            return add_row(source_row, sums)

        sums = lax.fori_loop(0, row, take, jnp.zeros((chunk, block), jnp.float32))
        wait_for(rs_recv.at[step, 0, pl.ds(0, n_col - 1)], rs_recv_sem.at[step, row])
        now = pols * (constant + add_row(row, sums))
        total = total + now

    stage[2] = now
    stage[3] = total
    for b in range(local_blocks):
        lanes = pl.ds(b * block, block)
        for c in range(3):
            at = 6 * b + 2 * c
            dip[c : c + 1, lanes] = stage[2, at : at + 1, :]
            grad[c : c + 1, lanes] = stage[3, at + 1 : at + 2, :]

    for step in range(ITERS):
        loop(0, row, lambda target: wait_for(ag_send.at[step], ag_send_sem.at[step, target]))
        wait_for(rs_recv.at[step, 0, pl.ds(0, n_col - 1)], rs_send_sem.at[step, row])
        loop(
            row + 1,
            n_row,
            lambda target: wait_for(
                rs_recv.at[step, 0, pl.ds(0, n_col)], rs_send_sem.at[step, target]
            ),
        )


def copy_out(*refs):
    count = (len(refs) - 1) // 2
    copies = [
        pltpu.make_async_copy(refs[i], refs[count + i], refs[-1].at[i]) for i in range(count)
    ]
    for copy in copies[::-1]:
        copy.start()
    for copy in copies:
        copy.wait()


def per_device(tensor_tiles, pair_blocks, polarizability, direct_field, cotangent):
    n_row = lax.axis_size("row")
    n_col = lax.axis_size("col")
    pair_count = tensor_tiles.shape[0]
    block = tensor_tiles.shape[2]
    local_blocks = polarizability.shape[0] // block
    chunk = -(-6 * local_blocks // 16) * 16
    f32, bf16 = jnp.float32, jnp.bfloat16
    tiles = tensor_tiles.transpose(0, 1, 3, 2, 4)
    vmem = pl.BlockSpec(memory_space=pltpu.VMEM)
    hbm = pl.BlockSpec(memory_space=pltpu.HBM)
    anywhere = pl.BlockSpec(memory_space=pl.ANY)
    dma = pltpu.SemaphoreType.DMA
    shapes = (
        jax.ShapeDtypeStruct(direct_field.shape, f32),
        jax.ShapeDtypeStruct(direct_field.shape, f32),
        jax.ShapeDtypeStruct(tiles.shape, bf16),
    )
    results = pl.pallas_call(
        functools.partial(kernel, n_row, n_col),
        out_shape=tuple(pltpu.VMEM(x.shape, x.dtype) for x in shapes),
        in_specs=[hbm] * 5,
        out_specs=(vmem,) * 3,
        scratch_shapes=[
            pltpu.VMEM(tiles.shape, bf16),
            pltpu.SMEM((2, pair_count), jnp.int32),
            pltpu.VMEM((local_blocks, block), f32),
            pltpu.VMEM(direct_field.shape, f32),
            pltpu.VMEM(direct_field.shape, f32),
            pltpu.VMEM((5, chunk, block), f32),
            pltpu.VMEM((ITERS, chunk, block), bf16),
            pltpu.VMEM((ITERS, n_row, chunk, block), bf16),
            pltpu.VMEM((ITERS, n_row, chunk, block), bf16),
            pltpu.VMEM((ITERS, n_row, n_col, chunk, block), bf16),
            pltpu.VMEM((ITERS, n_row * local_blocks, 8, block), f32),
            pltpu.VMEM((2 * pair_count, 8, block), f32),
            dma((pair_count,)),
            dma((4,)),
            dma((ITERS, n_row)),
            dma((ITERS, n_row)),
            dma((ITERS, n_row)),
            dma((ITERS, n_row)),
        ],
        compiler_params=pltpu.CompilerParams(
            collective_id=0, has_side_effects=True, vmem_limit_bytes=60 * 1024 * 1024
        ),
    )(
        tiles,
        pair_blocks.T,
        polarizability.reshape(local_blocks, block),
        direct_field,
        cotangent,
    )
    dipoles, grad, tile_grad = pl.pallas_call(
        copy_out,
        out_shape=shapes,
        in_specs=[vmem] * 3,
        out_specs=(anywhere,) * 3,
        scratch_shapes=[dma((3,))],
        compiler_params=pltpu.CompilerParams(vmem_limit_bytes=32 * 1024 * 1024),
    )(*results)
    return dipoles, grad, tile_grad.transpose(0, 1, 3, 2, 4)


def solution(mesh):
    placed = (
        P(("bead", "row", "col"), None, None, None, None),
        P(("bead", "row", "col"), None),
        P("row"),
        P(None, ("bead", "row")),
        P(None, ("bead", "row")),
    )
    return jax.shard_map(
        per_device,
        mesh=mesh,
        in_specs=placed,
        out_specs=(
            P(None, ("bead", "row")),
            P(None, ("bead", "row")),
            P(("bead", "row", "col"), None, None, None, None),
        ),
        check_vma=False,
    )
```

```python
import functools

import jax
import jax.numpy as jnp
from jax import lax
from jax.experimental import pallas as pl
from jax.experimental.pallas import tpu as pltpu
from jax.sharding import PartitionSpec as P

ITERS = 3
MESH = pl.DeviceIdType.MESH
UNROLL_LIMIT = 32


def repeat(count, step):
    if count <= UNROLL_LIMIT:
        for index in range(count):
            step(index)
    else:
        lax.fori_loop(0, count, lambda index, carry: (step(index), carry)[1], 0)


def loop(start, end, step):
    lax.fori_loop(start, end, lambda index, carry: (step(index), carry)[1], 0)


def kernel(
    n_row,
    n_col,
    tiles_hbm,
    pairs_hbm,
    pol_hbm,
    field_hbm,
    cot_hbm,
    dip,
    grad,
    tg,
    tiles,
    turned,
    pairs,
    pol,
    field_in,
    cot_in,
    stage,
    ag_send,
    ag_recv,
    rs_send,
    rs_recv,
    fields,
    part,
    tile_sem,
    in_sem,
    ag_send_sem,
    ag_recv_sem,
    rs_send_sem,
    rs_recv_sem,
):
    group = n_row * n_col
    pair_count = tiles.shape[0]
    block = tiles.shape[3]
    local_blocks = pol.shape[0]
    chunk = ag_send.shape[1]
    row = lax.axis_index("row")
    col = lax.axis_index("col")
    me = row * n_col + col

    inputs = [
        pltpu.make_async_copy(source, target, in_sem.at[index])
        for index, (source, target) in enumerate(
            ((pairs_hbm, pairs), (pol_hbm, pol), (field_hbm, field_in), (cot_hbm, cot_in))
        )
    ]
    tile_copies = [
        pltpu.make_async_copy(tiles_hbm.at[p], tiles.at[p], tile_sem.at[p])
        for p in range(pair_count)
    ]
    barrier = pltpu.get_barrier_semaphore()

    def far_first(index):
        return jnp.where(2 * col < n_col, n_col - 1 - index, index)

    def greet(index):
        other_row = lax.rem(row + n_row // 2 + index, n_row)
        for k in range(n_col):
            other_col = far_first(k)

            @pl.when((other_row != row) | (other_col != col))
            def _():
                pl.semaphore_signal(
                    barrier,
                    inc=1,
                    device_id={"row": other_row, "col": other_col},
                    device_id_type=MESH,
                )

    repeat(n_row, greet)
    for copy in inputs + tile_copies:
        copy.start()
    for copy in inputs:
        copy.wait()

    index = lax.broadcasted_iota(jnp.int32, (chunk, block), 0)
    even = lax.rem(index, 2) == 0
    stage[...] = jnp.zeros_like(stage)
    part[...] = jnp.zeros_like(part)
    for b in range(local_blocks):
        lanes = pl.ds(b * block, block)
        for c in range(3):
            at = 6 * b + 2 * c
            stage[0, at : at + 1, :] = field_in[c : c + 1, lanes]
            stage[0, at + 1 : at + 2, :] = cot_in[c : c + 1, lanes]
        stage[1, 6 * b : 6 * b + 6, :] = jnp.broadcast_to(pol[b : b + 1, :], (6, block))
    source = stage[0]
    pols = stage[1]
    now = pols * source
    total = now
    constant = jnp.where(even, source, 0.0)
    first = [pairs[0, p] for p in range(pair_count)]
    second = [pairs[1, p] for p in range(pair_count)]
    first_ids = [jnp.full((8, block), at, jnp.int32) for at in first]
    second_ids = [jnp.full((8, block), at, jnp.int32) for at in second]

    def wait_for(ref, semaphore):
        pltpu.make_async_copy(ref, ref, semaphore).wait()

    def vector(step, at):
        return jnp.concatenate(
            [fields[step, at, 2 * c : 2 * c + 2, :] for c in range(3)], axis=1
        )

    def unpack(step, which_row, packed):
        stage[2] = packed.astype(jnp.float32)
        for b in range(local_blocks):
            fields[step, which_row * local_blocks + b, 0:6, :] = stage[2, 6 * b : 6 * b + 6, :]

    def matrix(p, held):
        return jnp.concatenate(
            [
                jnp.concatenate([held[p, a, b] for b in range(3)], axis=1)
                for a in range(3)
            ],
            axis=0,
        )

    def keep(slot, values):
        for c in range(3):
            part[slot, 2 * c : 2 * c + 2, :] = values[:, c * block : (c + 1) * block]

    def summed(which_row, slots, ids):
        terms = [part[slot] for slot in slots]
        for b in range(local_blocks):
            at = which_row * local_blocks + b
            got = jnp.where(ids[0] == at, terms[0], 0.0)
            for term, which in zip(terms[1:], ids[1:]):
                got = got + jnp.where(which == at, term, 0.0)
            stage[3, 6 * b : 6 * b + 6, :] = got[0:6]
        return stage[3]

    def part_copy(step, target_row, target_col):
        return pltpu.make_async_remote_copy(
            src_ref=rs_send.at[step, target_row],
            dst_ref=rs_recv.at[step, row, col],
            send_sem=rs_send_sem.at[step, target_row],
            recv_sem=rs_recv_sem.at[step, row],
            device_id={"row": target_row, "col": target_col},
            device_id_type=MESH,
        )

    pl.semaphore_wait(barrier, group - 1)

    for step in range(ITERS):
        packed = now.astype(jnp.bfloat16)
        ag_send[step] = packed

        def send_field(target):
            pltpu.make_async_remote_copy(
                src_ref=ag_send.at[step],
                dst_ref=ag_recv.at[step, row],
                send_sem=ag_send_sem.at[step, target],
                recv_sem=ag_recv_sem.at[step, row],
                device_id={"row": target},
                device_id_type=MESH,
            ).start()

        loop(0, row, send_field)
        unpack(step, row, packed)

        for p in range(pair_count):
            if step == 0:
                tile_copies[p].wait()
            near = vector(step, first[p]).astype(jnp.bfloat16)
            keep(
                pair_count + p,
                lax.dot_general(
                    near,
                    matrix(p, tiles),
                    (((1,), (0,)), ((), ())),
                    preferred_element_type=jnp.float32,
                ),
            )

        def send_later(back):
            target = n_row - 1 - back
            later = summed(target, range(pair_count, 2 * pair_count), second_ids)
            rs_send[step, target] = later.astype(jnp.bfloat16)
            for k in range(n_col):
                part_copy(step, target, far_first(k)).start()

        loop(0, n_row - 1 - row, send_later)
        if step == 0:
            for p in range(pair_count):
                for a in range(3):
                    for b in range(3):
                        turned[p, b, a] = tiles[p, a, b].T

        stage[4] = summed(row, range(pair_count, 2 * pair_count), second_ids)

        def take_field(source_row):
            wait_for(ag_send.at[step], ag_recv_sem.at[step, source_row])
            unpack(step, source_row, ag_recv[step, source_row])

        loop(row + 1, n_row, take_field)
        for p in range(pair_count):
            far = vector(step, second[p]).astype(jnp.bfloat16)
            keep(
                p,
                lax.dot_general(
                    far,
                    matrix(p, turned),
                    (((1,), (0,)), ((), ())),
                    preferred_element_type=jnp.float32,
                ),
            )
        own = (stage[4] + summed(row, range(pair_count), first_ids)).astype(jnp.bfloat16)
        rs_send[step, row] = own
        for k in range(n_col):
            target_col = far_first(k)

            @pl.when(target_col != col)
            def _():
                part_copy(step, row, target_col).start()

        rs_recv[step, row, col] = own

        if step == ITERS - 1:
            for p in range(pair_count):
                left, right = [], []
                for t in range(ITERS):
                    left.append(vector(t, first[p]))
                    other = vector(ITERS - 1 - t, second[p])
                    right += [other[1:2], other[0:1]]
                blank = jnp.zeros((2, 3 * block), jnp.float32)
                left = jnp.concatenate(left + [blank], axis=0)
                right = jnp.concatenate(right + [blank], axis=0).astype(jnp.bfloat16)
                for a in range(3):
                    piece = left[:, a * block : (a + 1) * block].T.astype(jnp.bfloat16)
                    outer = jnp.dot(piece, right, preferred_element_type=jnp.float32)
                    for b in range(3):
                        tg[p, a, b] = outer[:, b * block : (b + 1) * block].astype(jnp.bfloat16)

        def add_row(source_row, sums):
            for c in range(n_col):
                sums = sums + rs_recv[step, source_row, c].astype(jnp.float32)
            return sums

        def take(source_row, sums):
            wait_for(
                rs_recv.at[step, 0, pl.ds(0, n_col)], rs_recv_sem.at[step, source_row]
            )
            return add_row(source_row, sums)

        sums = lax.fori_loop(0, row, take, jnp.zeros((chunk, block), jnp.float32))
        wait_for(rs_recv.at[step, 0, pl.ds(0, n_col - 1)], rs_recv_sem.at[step, row])
        now = pols * (constant + add_row(row, sums))
        total = total + now

    stage[2] = now
    stage[3] = total
    for b in range(local_blocks):
        lanes = pl.ds(b * block, block)
        for c in range(3):
            at = 6 * b + 2 * c
            dip[c : c + 1, lanes] = stage[2, at : at + 1, :]
            grad[c : c + 1, lanes] = stage[3, at + 1 : at + 2, :]

    for step in range(ITERS):
        loop(0, row, lambda target: wait_for(ag_send.at[step], ag_send_sem.at[step, target]))
        wait_for(rs_recv.at[step, 0, pl.ds(0, n_col - 1)], rs_send_sem.at[step, row])
        loop(
            row + 1,
            n_row,
            lambda target: wait_for(
                rs_recv.at[step, 0, pl.ds(0, n_col)], rs_send_sem.at[step, target]
            ),
        )


def copy_out(*refs):
    count = (len(refs) - 1) // 2
    copies = [
        pltpu.make_async_copy(refs[i], refs[count + i], refs[-1].at[i]) for i in range(count)
    ]
    for copy in copies[::-1]:
        copy.start()
    for copy in copies:
        copy.wait()


def per_device(tensor_tiles, pair_blocks, polarizability, direct_field, cotangent):
    n_row = lax.axis_size("row")
    n_col = lax.axis_size("col")
    pair_count = tensor_tiles.shape[0]
    block = tensor_tiles.shape[2]
    local_blocks = polarizability.shape[0] // block
    chunk = -(-6 * local_blocks // 16) * 16
    f32, bf16 = jnp.float32, jnp.bfloat16
    tiles = tensor_tiles.transpose(0, 1, 3, 2, 4)
    vmem = pl.BlockSpec(memory_space=pltpu.VMEM)
    hbm = pl.BlockSpec(memory_space=pltpu.HBM)
    anywhere = pl.BlockSpec(memory_space=pl.ANY)
    dma = pltpu.SemaphoreType.DMA
    shapes = (
        jax.ShapeDtypeStruct(direct_field.shape, f32),
        jax.ShapeDtypeStruct(direct_field.shape, f32),
        jax.ShapeDtypeStruct(tiles.shape, bf16),
    )
    results = pl.pallas_call(
        functools.partial(kernel, n_row, n_col),
        out_shape=tuple(pltpu.VMEM(x.shape, x.dtype) for x in shapes),
        in_specs=[hbm] * 5,
        out_specs=(vmem,) * 3,
        scratch_shapes=[
            pltpu.VMEM(tiles.shape, bf16),
            pltpu.VMEM(tiles.shape, bf16),
            pltpu.SMEM((2, pair_count), jnp.int32),
            pltpu.VMEM((local_blocks, block), f32),
            pltpu.VMEM(direct_field.shape, f32),
            pltpu.VMEM(direct_field.shape, f32),
            pltpu.VMEM((5, chunk, block), f32),
            pltpu.VMEM((ITERS, chunk, block), bf16),
            pltpu.VMEM((ITERS, n_row, chunk, block), bf16),
            pltpu.VMEM((ITERS, n_row, chunk, block), bf16),
            pltpu.VMEM((ITERS, n_row, n_col, chunk, block), bf16),
            pltpu.VMEM((ITERS, n_row * local_blocks, 8, block), f32),
            pltpu.VMEM((2 * pair_count, 8, block), f32),
            dma((pair_count,)),
            dma((4,)),
            dma((ITERS, n_row)),
            dma((ITERS, n_row)),
            dma((ITERS, n_row)),
            dma((ITERS, n_row)),
        ],
        compiler_params=pltpu.CompilerParams(
            collective_id=0, has_side_effects=True, vmem_limit_bytes=60 * 1024 * 1024
        ),
    )(
        tiles,
        pair_blocks.T,
        polarizability.reshape(local_blocks, block),
        direct_field,
        cotangent,
    )
    dipoles, grad, tile_grad = pl.pallas_call(
        copy_out,
        out_shape=shapes,
        in_specs=[vmem] * 3,
        out_specs=(anywhere,) * 3,
        scratch_shapes=[dma((3,))],
        compiler_params=pltpu.CompilerParams(vmem_limit_bytes=32 * 1024 * 1024),
    )(*results)
    return dipoles, grad, tile_grad.transpose(0, 1, 3, 2, 4)


def solution(mesh):
    placed = (
        P(("bead", "row", "col"), None, None, None, None),
        P(("bead", "row", "col"), None),
        P("row"),
        P(None, ("bead", "row")),
        P(None, ("bead", "row")),
    )
    return jax.shard_map(
        per_device,
        mesh=mesh,
        in_specs=placed,
        out_specs=(
            P(None, ("bead", "row")),
            P(None, ("bead", "row")),
            P(("bead", "row", "col"), None, None, None, None),
        ),
        check_vma=False,
    )
```
